256 devices in a mesh: hist: 8 (over z), cand: 32 (over x, y, core).
Axes of the slice: x: 4, y: 4, z: 8, core: 2. Of those that a mesh axis runs over, the one named last changes fastest.
Arguments:
- candidates: bfloat16 [32, 256, 1024], P('cand'), may hold values from -6 to 6
- input_gain: float32 [1024], replicated, may hold values from 0.1 to 1.9
- proj_weight: bfloat16 [2, 1024, 1024], P(None, None, 'hist'), may hold values from -0.1875 to 0.1875
- history_cache: bfloat16 [1280, 8, 512, 256], P('cand', 'hist'), may hold values from -6 to 6
- slot_user: int32 [1280], P('cand'), may hold values from 0 to 31
- slot_block: int32 [1280], P('cand'), may hold values from -1 to 31, as said below
- history_len: int32 [32], replicated, may hold values from 1537 to 16384
- attention_gain: float32 [1024], replicated, may hold values from 0.1 to 1.9
- out_weight: bfloat16 [1024, 1024], P(None, 'hist'), may hold values from -0.1875 to 0.1875
Outputs:
- result: bfloat16 [32, 256, 1024], P('cand', None, 'hist')
The draws below stay inside these ranges and needn't reach their ends.
Inputs may be any that keep to these rules, and one draw needn't show every extreme that they name: Each pair of a user u and a block number b < ceil(history_len[u] / 512) is held by exactly one slot; every other slot has slot_block -1.
All inputs are finite; a program needn't handle non-finite values.
Results may differ from the reference program's by a relative error of at most 0.015.
Values may be sent and summed in bfloat16 or wider, within the bound.
A program may use at most 128 MiB of HBM per device.

```python
import jax
import jax.numpy as jnp
from jax import lax

D = 1024
H = 8
DH = 128
BLK = 512
CANDS = 256
MAXB = 32
USERS = 32
SLOTS = 1280


def block_layout(key):
    keys = jax.random.split(key, 5)
    lowest = max(1, MAXB // 8)
    blocks = jax.random.randint(keys[0], (USERS,), lowest, MAXB + 1)
    extra = jax.random.randint(keys[1], (USERS,), 0, BLK)
    lengths = (blocks - 1) * BLK + 1 + extra
    longest = jax.random.randint(keys[2], (), 0, USERS)
    user_ids = jnp.arange(USERS, dtype=jnp.int32)
    lengths = jnp.where(user_ids == longest, MAXB * BLK, lengths)
    blocks = jnp.where(user_ids == longest, MAXB, blocks)
    entry = jnp.arange(SLOTS, dtype=jnp.int32)
    entry_user = jnp.minimum(entry // MAXB, USERS - 1)
    entry_block = entry % MAXB
    filler_user = jax.random.randint(keys[3], (SLOTS,), 0, USERS)
    in_table = entry < USERS * MAXB
    owner_blocks = jnp.sum(jnp.where(entry_user[:, None] == user_ids[None, :], blocks[None, :], 0), axis=1)
    is_live = in_table & (entry_block < owner_blocks)
    user_of_entry = jnp.where(in_table, entry_user, filler_user)
    block_of_entry = jnp.where(is_live, entry_block, -1)
    order = jax.random.permutation(keys[4], SLOTS)
    slot_users = jnp.zeros((SLOTS,), jnp.int32).at[order].set(user_of_entry.astype(jnp.int32))
    slot_blocks = jnp.zeros((SLOTS,), jnp.int32).at[order].set(block_of_entry.astype(jnp.int32))
    return (lengths.astype(jnp.int32), slot_users, slot_blocks)


def draw_slot_user(key, part):
    lengths, slot_users, slot_blocks = block_layout(key)
    return slot_users


def draw_slot_block(key, part):
    lengths, slot_users, slot_blocks = block_layout(key)
    return slot_blocks


def draw_history_len(key, part):
    lengths, slot_users, slot_blocks = block_layout(key)
    return lengths


def steps_of(stream_key, shape, cuts, least, high):
    def one(dim, blocks):
        steps = jax.random.uniform(jax.random.fold_in(jax.random.fold_in(stream_key, 6), dim), (blocks,), jnp.float32, least / len(cuts), high / len(cuts))
        return jnp.repeat(jnp.exp(steps), shape[dim] // blocks).reshape((-1,) + (1,) * (len(shape) - dim - 1))

    level = one(*cuts[0])
    for cut in cuts[1:]:
        level = level * one(*cut)
    return level


def scatter_about(rng, extent, spread, reach, shards=(), kind=jnp.bfloat16):
    loudness = steps_of(rng, extent, shards, -0.22, 0.18) if shards else 1.0
    entries = jax.random.normal(rng, extent, jnp.float32) * spread * loudness
    return jnp.minimum(jnp.maximum(entries, -reach), reach).astype(kind)


def setup_inputs(seed: int = 0) -> dict:
    key_of = jax.random.split(jax.random.key(seed), 10)
    candidates = scatter_about(key_of[0], (USERS, CANDS, D), 1.0, 6.0, ((0, 32),))
    input_gain = jnp.clip(1.0 + 0.18 * jax.random.normal(key_of[1], (D,), jnp.float32), 0.1, 1.9)
    proj_weight = scatter_about(key_of[2], (2, D, D), D ** -0.5, 0.1875, ((2, 8),))
    history_cache = scatter_about(key_of[3], (SLOTS, H, BLK, 2 * DH), 1.0, 6.0, ((0, 32), (1, 8)))
    slot_user = draw_slot_user(jax.random.fold_in(key_of[9], 71), 0)
    slot_block = draw_slot_block(jax.random.fold_in(key_of[9], 71), 0)
    history_len = draw_history_len(jax.random.fold_in(key_of[9], 71), 0)
    attention_gain = jnp.clip(1.0 + 0.18 * jax.random.normal(key_of[7], (D,), jnp.float32), 0.1, 1.9)
    out_weight = scatter_about(key_of[8], (D, D), D ** -0.5, 0.1875, ((1, 8),))
    return {"candidates": candidates, "input_gain": input_gain, "proj_weight": proj_weight, "history_cache": history_cache, "slot_user": slot_user, "slot_block": slot_block, "history_len": history_len, "attention_gain": attention_gain, "out_weight": out_weight}


def layer_norm(rows, gain):
    row_mean = lax.optimization_barrier(jnp.mean(rows, axis=-1, keepdims=True))
    centred = rows - row_mean
    row_var = lax.optimization_barrier(jnp.mean(centred * centred, axis=-1, keepdims=True))
    return centred * lax.rsqrt(row_var + 1e-05) * gain

def reference(candidates, input_gain, proj_weight, history_cache, slot_user, slot_block, history_len, attention_gain, out_weight):
    cand_rows = candidates.astype(jnp.float32)
    normed_input = layer_norm(cand_rows, input_gain.astype(jnp.float32)).astype(jnp.bfloat16)
    flat_rows = normed_input.reshape(USERS * CANDS, D)
    gate_all = jax.nn.silu(jnp.dot(flat_rows, proj_weight[0], preferred_element_type=jnp.float32)).astype(jnp.bfloat16).reshape(USERS, CANDS, D)
    query_all = jax.nn.silu(jnp.dot(flat_rows, proj_weight[1], preferred_element_type=jnp.float32)).astype(jnp.bfloat16).reshape(USERS, CANDS, D)
    event_index = jnp.arange(BLK, dtype=jnp.int32)
    score_scale = DH ** (-0.5)

    def add_slot(carry, items):
        cache_block, owner, position = items
        query = lax.dynamic_index_in_dim(query_all, owner, 0, keepdims=False).astype(jnp.float32).reshape(CANDS, H, DH)
        cache_keys = cache_block[..., :DH].astype(jnp.float32)
        cache_values = cache_block[..., DH:].astype(jnp.float32)
        scores = jnp.einsum('chd,htd->hct', query, cache_keys) * score_scale
        length = lax.dynamic_index_in_dim(history_len, owner, 0, keepdims=False)
        live_mask = (position >= 0) & (position * BLK + event_index < length)
        weights = (jax.nn.silu(scores) * live_mask.astype(jnp.float32)).astype(jnp.bfloat16)
        weights = lax.optimization_barrier(weights).astype(jnp.float32)
        contrib = jnp.einsum('hct,htd->chd', weights, cache_values).reshape(CANDS, D)
        current = lax.dynamic_index_in_dim(carry, owner, 0, keepdims=False)
        carry = lax.dynamic_update_index_in_dim(carry, current + contrib, owner, 0)
        return (carry, None)
    attention, _ = lax.scan(add_slot, jnp.zeros((USERS, CANDS, D), jnp.float32), (history_cache, slot_user, slot_block))
    gated = (layer_norm(attention, attention_gain.astype(jnp.float32)) * gate_all.astype(jnp.float32)).astype(jnp.bfloat16)
    result = cand_rows + jnp.dot(gated.reshape(USERS * CANDS, D), out_weight, preferred_element_type=jnp.float32).reshape(USERS, CANDS, D)
    return result.astype(jnp.bfloat16)
```

```python
import functools

import jax
import jax.numpy as jnp
from jax import lax
from jax.experimental import pallas as pl
from jax.experimental.pallas import tpu as pltpu
from jax.sharding import PartitionSpec as P

D = 1024
DH = 128
CANDS = 256
HALF = CANDS // 2
BLK = 512
SLOTS_HERE = 40
USERS = 32
NX, NY, NZ = 4, 4, 8
GROUP = 4
F32 = jnp.float32
BF16 = jnp.bfloat16
MESH = pl.DeviceIdType.MESH
HALF_SCALE = 0.5 * DH ** (-0.5)


def place():
    cand = lax.axis_index("cand")
    return cand // (2 * NY), (cand // 2) % NY, cand % 2, lax.axis_index("hist")


def device(x, y, c, z):
    return (z, (x * NY + y) * 2 + c)


def greet(x, y, c, z):
    barrier = pltpu.get_barrier_semaphore()
    peers = [device(x, y, 1 - c, z)]
    peers += [device((x + d) % NX, y, c, z) for d in range(1, NX)]
    peers += [device(x, (y + d) % NY, c, z) for d in range(1, NY)]
    peers += [device(x, y, c, (z + d) % NZ) for d in range(1, NZ)]
    for peer in peers:
        pl.semaphore_signal(barrier, inc=1, device_id=peer, device_id_type=MESH)
    return barrier, len(peers)


def remote(src, dst, send_sem, recv_sem, peer):
    return pltpu.make_async_remote_copy(
        src_ref=src,
        dst_ref=dst,
        send_sem=send_sem,
        recv_sem=recv_sem,
        device_id=peer,
        device_id_type=MESH,
    )


def silu(value):
    half = 0.5 * value
    return half + half * jnp.tanh(half)


def layer_norm(rows, gain):
    centred = rows - jnp.mean(rows, axis=-1, keepdims=True)
    row_var = jnp.mean(centred * centred, axis=-1, keepdims=True)
    return centred * lax.rsqrt(row_var + 1e-05) * gain


def query_kernel(
    cand_hbm,
    gain_hbm,
    proj_hbm,
    query_all,
    gate_all,
    cand_cols,
    cand_rows,
    gain,
    proj,
    normed,
    load_sem,
    line_send,
    line_recv,
    cross_send,
    cross_recv,
    core_send,
    core_recv,
    gate_send,
    gate_recv,
):
    x, y, c, z = place()
    barrier, greeted = greet(x, y, c, z)
    loads = [
        pltpu.make_async_copy(cand_hbm.at[0], cand_rows, load_sem.at[0]),
        pltpu.make_async_copy(gain_hbm, gain, load_sem.at[1]),
        pltpu.make_async_copy(proj_hbm, proj, load_sem.at[2]),
    ]
    for load in loads:
        load.start()
    loads[0].wait()
    loads[1].wait()
    for part in range(4):
        rows = pl.ds(part * 64, 64)
        normed[rows, :] = layer_norm(cand_rows[rows, :].astype(F32), gain[...]).astype(BF16)
    loads[2].wait()
    query_all[x, y, c] = silu(
        jnp.dot(normed[...], proj[1], preferred_element_type=F32)
    ).astype(BF16)
    pl.semaphore_wait(barrier, greeted)

    halves = [pl.ds(0, HALF), pl.ds(HALF, HALF)]
    sends = []
    line = [[], []]
    for d in (2, 1, 3):
        for h in range(2):
            peer = device((x + d) % NX, y, c, z) if h == 0 else device(x, (y + d) % NY, c, z)
            own = query_all.at[x, y, c, halves[h]]
            copy = remote(own, own, line_send.at[h, d], line_recv.at[h, d], peer)
            copy.start()
            line[h].append(copy)
            sends.append(copy)

    gate_all[z] = silu(
        jnp.dot(normed[...], proj[0], preferred_element_type=F32)
    ).astype(BF16)
    gates = []
    for d in (4, 3, 5, 2, 6, 1, 7):
        own = gate_all.at[z]
        copy = remote(
            own, own, gate_send.at[d], gate_recv.at[d], device(x, y, c, (z + d) % NZ)
        )
        copy.start()
        gates.append(copy)
        sends.append(copy)

    cand_cols[...] = cand_rows[:, pl.ds(pl.multiple_of(z * DH, DH), DH)]

    cross = [[], []]
    core = []

    def to_core(index, block):
        copy = remote(
            block, block, core_send.at[index], core_recv.at[index], device(x, y, 1 - c, z)
        )
        copy.start()
        core.append(copy)
        sends.append(copy)

    for h in range(2):
        for copy in line[h]:
            copy.wait_recv()
        for d in (2, 1, 3):
            if h == 0:
                block = query_all.at[:, y, c, halves[h]]
                peer = device(x, (y + d) % NY, c, z)
            else:
                block = query_all.at[x, :, c, halves[h]]
                peer = device((x + d) % NX, y, c, z)
            copy = remote(block, block, cross_send.at[h, d], cross_recv.at[h, d], peer)
            copy.start()
            cross[h].append((d, copy))
            sends.append(copy)
        to_core(h, block)

    for turn in (1, 2, 0):
        for h in range(2):
            d, copy = cross[h][turn]
            copy.wait_recv()
            if h == 0:
                block = query_all.at[:, (y + NY - d) % NY, c, halves[h]]
            else:
                block = query_all.at[(x + NX - d) % NX, :, c, halves[h]]
            to_core(2 + 2 * turn + h, block)
    for copy in gates:
        copy.wait_recv()
    for copy in core:
        copy.wait_recv()
    for copy in sends:
        copy.wait_send()


def attention_kernel(
    user_hbm,
    block_hbm,
    length_hbm,
    query_all,
    cache_hbm,
    partial,
    total,
    cache,
    user_ref,
    block_ref,
    length_ref,
    slots,
    counts,
    load_sem,
    sems,
):
    loads = [
        pltpu.make_async_copy(user_hbm, user_ref, load_sem.at[0]),
        pltpu.make_async_copy(block_hbm, block_ref, load_sem.at[1]),
        pltpu.make_async_copy(length_hbm, length_ref, load_sem.at[2]),
    ]
    for load in loads:
        load.start()
    for load in loads:
        load.wait()

    def find(slot, found):
        user = user_ref[slot]
        block = block_ref[slot]
        count = jnp.clip(length_ref[user] - block * BLK, 0, BLK)
        live = (block >= 0) & (count > 0)

        @pl.when(live)
        def _():
            slots[found] = slot
            counts[found] = count
            pltpu.make_async_copy(cache_hbm.at[slot, 0], cache.at[slot], sems.at[slot]).start()

        return found + live.astype(jnp.int32)

    found = lax.fori_loop(0, SLOTS_HERE, find, 0)
    for extra in range(GROUP - 1):
        slots[found + extra] = slots[0]
        counts[found + extra] = 0

    def clear(user, _):
        total[user] = jnp.zeros((CANDS, DH), F32)
        return 0

    lax.fori_loop(0, USERS, clear, 0)
    event = lax.broadcasted_iota(jnp.int32, (1, BLK), 1)

    def group(first, _):
        for step in range(GROUP):
            entry = first * GROUP + step
            slot = slots[entry]

            @pl.when(entry < found)
            def _(slot=slot):
                pltpu.make_async_copy(cache_hbm.at[slot, 0], cache.at[slot], sems.at[slot]).wait()

        sums = []
        for step in range(GROUP):
            entry = first * GROUP + step
            slot = slots[entry]
            user = user_ref[slot]
            scale = jnp.where(event < counts[entry], HALF_SCALE, 0.0)
            scores = lax.dot_general(
                query_all[user],
                cache[slot, :, :DH],
                (((1,), (1,)), ((), ())),
                preferred_element_type=F32,
            )
            half = scores * scale
            weights = (half + half * jnp.tanh(half)).astype(BF16)
            sums.append(
                (user, jnp.dot(weights, cache[slot, :, DH:], preferred_element_type=F32))
            )
        for user, value in sums:
            total[user] += value
        return 0

    lax.fori_loop(0, (found + GROUP - 1) // GROUP, group, 0)

    def store(user, _):
        partial[user] = total[user].astype(BF16)
        return 0

    lax.fori_loop(0, USERS, store, 0)


def output_kernel(
    partial,
    gate_all,
    cand_cols,
    gain_hbm,
    weight_hbm,
    result,
    core_in,
    cross_out,
    cross_in,
    line_out,
    line_in,
    attention,
    gain,
    weight,
    load_sem,
    core_send,
    core_recv,
    cross_send,
    cross_recv,
    line_send,
    line_recv,
    head_send,
    head_recv,
):
    x, y, c, z = place()
    barrier, greeted = greet(x, y, c, z)
    loads = [
        pltpu.make_async_copy(gain_hbm, gain, load_sem.at[0]),
        pltpu.make_async_copy(weight_hbm, weight, load_sem.at[1]),
    ]
    for load in loads:
        load.start()
    pl.semaphore_wait(barrier, greeted)

    halves = [pl.ds(0, HALF), pl.ds(HALF, HALF)]
    sends = []
    core = {}

    def lot(h, d, core_index):
        if h == 0:
            return partial.at[:, (y + d) % NY, core_index, halves[h]]
        return partial.at[(x + d) % NX, :, core_index, halves[h]]

    order = (2, 1, 3, 0)
    for d in order:
        for h in range(2):
            copy = remote(
                lot(h, d, 1 - c),
                core_in.at[h, d],
                core_send.at[h, d],
                core_recv.at[h, d],
                device(x, y, 1 - c, z),
            )
            copy.start()
            core[h, d] = copy
            sends.append(copy)
    cross = {}
    for d in order:
        for h in range(2):
            core[h, d].wait_recv()
            summed = lot(h, d, c)[...].astype(F32) + core_in[h, d].astype(F32)
            cross_out[h, d] = summed.astype(BF16)
            if d:
                peer = device(x, (y + d) % NY, c, z) if h == 0 else device((x + d) % NX, y, c, z)
                copy = remote(
                    cross_out.at[h, d],
                    cross_in.at[h, d],
                    cross_send.at[h, d],
                    cross_recv.at[h, d],
                    peer,
                )
                copy.start()
                cross[h, d] = copy
                sends.append(copy)
    line = {}
    for h in range(2):
        for d in (1, 3, 2):
            cross[h, d].wait_recv()
        own = x if h == 0 else y
        for d in order:
            other = (own + d) % NX
            value = cross_out[h, 0, other].astype(F32)
            for e in range(1, NX):
                value += cross_in[h, e, other].astype(F32)
            line_out[h, d] = value.astype(BF16)
            if d:
                peer = device(other, y, c, z) if h == 0 else device(x, other, c, z)
                copy = remote(
                    line_out.at[h, d],
                    line_in.at[h, d],
                    line_send.at[h, d],
                    line_recv.at[h, d],
                    peer,
                )
                copy.start()
                line[h, d] = copy
                sends.append(copy)
    head = {}
    for h in range(2):
        value = line_out[h, 0].astype(F32)
        for d in (1, 3, 2):
            line[h, d].wait_recv()
            value += line_in[h, d].astype(F32)
        attention[h, z] = value.astype(BF16)
        for d in (4, 3, 5, 2, 6, 1, 7):
            own = attention.at[h, z]
            copy = remote(
                own, own, head_send.at[h, d], head_recv.at[h, d], device(x, y, c, (z + d) % NZ)
            )
            copy.start()
            head[h, d] = copy
            sends.append(copy)
    for load in loads:
        load.wait()
    for h in range(2):
        for d in range(1, NZ):
            head[h, d].wait_recv()
        for part in range(2):
            rows = pl.ds(part * 64, 64)
            out_rows = pl.ds(h * HALF + part * 64, 64)
            whole = jnp.concatenate(
                [attention[h, k, rows].astype(F32) for k in range(NZ)], axis=1
            )
            gates = jnp.concatenate(
                [gate_all[k, out_rows].astype(F32) for k in range(NZ)], axis=1
            )
            gated = (layer_norm(whole, gain[...]) * gates).astype(BF16)
            projected = jnp.dot(gated, weight[...], preferred_element_type=F32)
            result[0, out_rows, :] = (cand_cols[out_rows, :].astype(F32) + projected).astype(BF16)
    for copy in sends:
        copy.wait_send()


def local(
    candidates,
    input_gain,
    proj_weight,
    history_cache,
    slot_user,
    slot_block,
    history_len,
    attention_gain,
    out_weight,
):
    dma = pltpu.SemaphoreType.DMA
    vmem = pl.BlockSpec(memory_space=pltpu.VMEM)
    anywhere = pl.BlockSpec(memory_space=pl.ANY)
    in_hbm = functools.partial(pltpu.with_memory_space_constraint, memory_space=pltpu.HBM)
    query_all, gate_all, cand_cols = pl.pallas_call(
        query_kernel,
        out_shape=[
            pltpu.VMEM((NX, NY, 2, CANDS, DH), BF16),
            pltpu.VMEM((NZ, CANDS, DH), BF16),
            pltpu.VMEM((CANDS, DH), BF16),
        ],
        in_specs=[anywhere] * 3,
        out_specs=[vmem] * 3,
        scratch_shapes=[
            pltpu.VMEM((CANDS, D), BF16),
            pltpu.VMEM((1, D), F32),
            pltpu.VMEM((2, D, DH), BF16),
            pltpu.VMEM((CANDS, D), BF16),
            dma((3,)),
            dma((2, NX)),
            dma((2, NX)),
            dma((2, NX)),
            dma((2, NX)),
            dma((8,)),
            dma((8,)),
            dma((NZ,)),
            dma((NZ,)),
        ],
        compiler_params=pltpu.CompilerParams(
            collective_id=0, has_side_effects=True, vmem_limit_bytes=24 << 20
        ),
        name="query",
    )(in_hbm(candidates), in_hbm(input_gain.reshape(1, D)), in_hbm(proj_weight))

    partial = pl.pallas_call(
        attention_kernel,
        out_shape=pltpu.VMEM((USERS, CANDS, DH), BF16),
        in_specs=[anywhere] * 3 + [vmem, anywhere],
        out_specs=vmem,
        scratch_shapes=[
            pltpu.VMEM((USERS, CANDS, DH), F32),
            pltpu.VMEM((SLOTS_HERE, BLK, 2 * DH), BF16),
            pltpu.SMEM((SLOTS_HERE,), jnp.int32),
            pltpu.SMEM((SLOTS_HERE,), jnp.int32),
            pltpu.SMEM((USERS,), jnp.int32),
            pltpu.SMEM((SLOTS_HERE + GROUP,), jnp.int32),
            pltpu.SMEM((SLOTS_HERE + GROUP,), jnp.int32),
            dma((3,)),
            dma((SLOTS_HERE,)),
        ],
        compiler_params=pltpu.CompilerParams(vmem_limit_bytes=32 << 20),
        name="attention",
    )(
        in_hbm(slot_user),
        in_hbm(slot_block),
        in_hbm(history_len),
        query_all.reshape(USERS, CANDS, DH),
        in_hbm(history_cache),
    )

    return pl.pallas_call(
        output_kernel,
        out_shape=jax.ShapeDtypeStruct((1, CANDS, DH), BF16),
        in_specs=[vmem] * 3 + [anywhere] * 2,
        out_specs=vmem,
        scratch_shapes=[
            pltpu.VMEM((2, NX, NX, HALF, DH), BF16),
            pltpu.VMEM((2, NX, NX, HALF, DH), BF16),
            pltpu.VMEM((2, NX, NX, HALF, DH), BF16),
            pltpu.VMEM((2, NX, HALF, DH), BF16),
            pltpu.VMEM((2, NX, HALF, DH), BF16),
            pltpu.VMEM((2, NZ, HALF, DH), BF16),
            pltpu.VMEM((1, D), F32),
            pltpu.VMEM((D, DH), BF16),
            dma((2,)),
            dma((2, NX)),
            dma((2, NX)),
            dma((2, NX)),
            dma((2, NX)),
            dma((2, NX)),
            dma((2, NX)),
            dma((2, NZ)),
            dma((2, NZ)),
        ],
        compiler_params=pltpu.CompilerParams(
            collective_id=1, has_side_effects=True, vmem_limit_bytes=24 << 20
        ),
        name="output",
    )(
        partial.reshape(NX, NY, 2, CANDS, DH),
        gate_all,
        cand_cols,
        in_hbm(attention_gain.reshape(1, D)),
        in_hbm(out_weight),
    )


def solution(mesh):
    return jax.shard_map(
        local,
        mesh=mesh,
        in_specs=(
            P("cand", None, None),
            P(),
            P(None, None, "hist"),
            P("cand", "hist", None, None),
            P("cand"),
            P("cand"),
            P(),
            P(),
            P(None, "hist"),
        ),
        out_specs=P("cand", None, "hist"),
        check_vma=False,
    )
```

```python
import functools

import jax
import jax.numpy as jnp
from jax import lax
from jax.experimental import pallas as pl
from jax.experimental.pallas import tpu as pltpu
from jax.sharding import PartitionSpec as P

D = 1024
DH = 128
CANDS = 256
HALF = CANDS // 2
QUARTER = CANDS // 4
BLK = 512
TILE = 256
SLOTS_HERE = 40
USERS = 32
NX, NY, NZ = 4, 4, 8
UNROLL = 4
ROUNDS = SLOTS_HERE // (2 * UNROLL)
F32 = jnp.float32
BF16 = jnp.bfloat16
I32 = jnp.int32
MESH = pl.DeviceIdType.MESH
HALF_SCALE = 0.5 * DH ** (-0.5)
FAR_FIRST = (2, 1, 3, 0)
HEADS_FAR_FIRST = (4, 3, 5, 2, 6, 1, 7)
SLOT, OWNER, COUNT, SAME, LAST = range(5)


def place():
    cand = lax.axis_index("cand")
    return cand // (2 * NY), (cand // 2) % NY, cand % 2, lax.axis_index("hist")


def device(x, y, c, z):
    return (z, (x * NY + y) * 2 + c)


def remote(src, dst, send_sem, recv_sem, peer):
    return pltpu.make_async_remote_copy(
        src_ref=src,
        dst_ref=dst,
        send_sem=send_sem,
        recv_sem=recv_sem,
        device_id=peer,
        device_id_type=MESH,
    )


def silu(value):
    half = 0.5 * value
    return half + half * jnp.tanh(half)


def layer_norm(rows, gain):
    centred = rows - jnp.mean(rows, axis=-1, keepdims=True)
    row_var = jnp.mean(centred * centred, axis=-1, keepdims=True)
    return centred * lax.rsqrt(row_var + 1e-05) * gain


def sort_slots(user_row, block_row, length_row, table):
    shape = (SLOTS_HERE, SLOTS_HERE)
    row_id = lax.broadcasted_iota(I32, shape, 0)
    col_id = lax.broadcasted_iota(I32, shape, 1)
    diagonal = row_id == col_id
    slot = lax.broadcasted_iota(I32, (SLOTS_HERE, 1), 0)
    user_id = lax.broadcasted_iota(I32, (SLOTS_HERE, USERS), 1)

    def across(mask, value):
        return jnp.sum(jnp.where(mask, value, 0), axis=1, keepdims=True)

    def down(mask, value):
        return jnp.sum(jnp.where(mask, value, 0), axis=0, keepdims=True)

    user = across(diagonal, user_row)
    block = across(diagonal, block_row)
    length = across(user_id == user, length_row)
    count = jnp.clip(length - block * BLK, 0, BLK)
    live = (block >= 0) & (count > 0)
    key = jnp.where(live, user * SLOTS_HERE, USERS * SLOTS_HERE) + slot
    key_row = down(diagonal, key)
    rank = across(key_row < key, 1)
    here = rank == col_id
    owner = down(here, user)
    before = down(rank + 1 == col_id, user + 1)
    through = down(live & (user <= user_id), 1)
    mine = down(live & (user == user_id), 1)
    table[...] = jnp.zeros_like(table)
    table[SLOT : SLOT + 1, :SLOTS_HERE] = down(here, slot)
    table[OWNER : OWNER + 1, :SLOTS_HERE] = owner
    table[COUNT : COUNT + 1, :SLOTS_HERE] = down(here, jnp.where(live, count, 0))
    table[SAME : SAME + 1, :SLOTS_HERE] = (before == owner + 1).astype(I32)
    table[LAST : LAST + 1, :USERS] = jnp.where(mine > 0, through - 1, SLOTS_HERE)


def attend(table, query, cache, sums, total, first, last):
    event = lax.broadcasted_iota(I32, (1, BLK), 1)
    blank = jnp.zeros((HALF, DH), BF16)

    def weigh(scores, scale):
        half = scores * scale
        return (half + half * jnp.tanh(half)).astype(BF16)

    def step(round_id, _):
        for turn in range(UNROLL):
            entry = (round_id * UNROLL + turn) * 2
            slot_a, slot_b = table[SLOT, entry], table[SLOT, entry + 1]
            scale_a = jnp.where(event < table[COUNT, entry], HALF_SCALE, 0.0)
            scale_b = jnp.where(event < table[COUNT, entry + 1], HALF_SCALE, 0.0)
            queries = jnp.concatenate(
                [
                    jnp.concatenate([query[table[OWNER, entry]], blank], axis=1),
                    jnp.concatenate([blank, query[table[OWNER, entry + 1]]], axis=1),
                ],
                axis=0,
            )
            value = jnp.zeros((2 * HALF, 2 * DH), F32)
            for tile in range(BLK // TILE):
                cols = slice(tile * TILE, (tile + 1) * TILE)
                keys = jnp.concatenate(
                    [cache[slot_a, cols, :DH], cache[slot_b, cols, :DH]], axis=1
                )
                values = jnp.concatenate(
                    [cache[slot_a, cols, DH:], cache[slot_b, cols, DH:]], axis=1
                )
                scores = lax.dot_general(
                    queries, keys, (((1,), (1,)), ((), ())), preferred_element_type=F32
                )
                weights = jnp.concatenate(
                    [weigh(scores[:HALF], scale_a[:, cols]), weigh(scores[HALF:], scale_b[:, cols])],
                    axis=0,
                )
                value += jnp.dot(weights, values, preferred_element_type=F32)
            run = total[...] * table[SAME, entry].astype(F32) + value[:HALF, :DH]
            sums[entry] = run.astype(BF16)
            run = run * table[SAME, entry + 1].astype(F32) + value[HALF:, DH:]
            sums[entry + 1] = run.astype(BF16)
            total[...] = run
        return 0

    lax.fori_loop(first, last, step, 0)


def kernel(
    cand_hbm,
    input_gain_hbm,
    proj_hbm,
    cache_hbm,
    user_hbm,
    block_hbm,
    length_hbm,
    attention_gain_hbm,
    weight_hbm,
    result,
    cand_rows,
    input_gain,
    proj,
    cache,
    user_row,
    block_row,
    length_row,
    attention_gain,
    weight,
    normed,
    query_a,
    query_b,
    gate_all,
    table_rows,
    table,
    sums_a,
    sums_b,
    total,
    core_out,
    core_in,
    peer_out,
    peer_in,
    attention,
    load_sem,
    line_send,
    line_recv,
    cross_send,
    cross_recv,
    share_send,
    share_recv,
    gate_send,
    gate_recv,
    core_send,
    core_recv,
    peer_send,
    peer_recv,
    head_send,
    head_recv,
):
    x, y, c, z = place()
    barrier = pltpu.get_barrier_semaphore()
    peers = [device(x, y, 1 - c, z)]
    peers += [
        device((x + dx) % NX, (y + dy) % NY, c, z)
        for dx in range(NX)
        for dy in range(NY)
        if dx or dy
    ]
    peers += [device(x, y, c, (z + d) % NZ) for d in range(1, NZ)]
    for peer in peers:
        pl.semaphore_signal(barrier, inc=1, device_id=peer, device_id_type=MESH)

    pairs = [
        (cand_hbm.at[0], cand_rows),
        (input_gain_hbm, input_gain),
        (proj_hbm, proj),
        (user_hbm, user_row),
        (block_hbm, block_row),
        (length_hbm, length_row),
        (cache_hbm.at[:, 0], cache),
        (attention_gain_hbm, attention_gain),
        (weight_hbm, weight),
    ]
    loads = [
        pltpu.make_async_copy(src, dst, load_sem.at[i]) for i, (src, dst) in enumerate(pairs)
    ]
    for load in loads:
        load.start()

    query = (query_a, query_b)
    sums = (sums_a, sums_b)
    halves = (pl.ds(0, HALF), pl.ds(HALF, HALF))
    quarters = (pl.ds(0, QUARTER), pl.ds(QUARTER, QUARTER))
    sends = []

    def go(src, dst, send_sem, recv_sem, peer):
        copy = remote(src, dst, send_sem, recv_sem, peer)
        copy.start()
        sends.append(copy)
        return copy

    def project_query(h):
        for part in range(2):
            rows = pl.ds(h * HALF + part * QUARTER, QUARTER)
            normed[rows, :] = layer_norm(
                cand_rows[rows, :].astype(F32), input_gain[...]
            ).astype(BF16)
        if h == 0:
            loads[2].wait()
        query[h][x, y, c] = silu(
            jnp.dot(normed[halves[h], :], proj[1], preferred_element_type=F32)
        ).astype(BF16)

    line, cross, share = {}, {}, {}

    def send_line(h):
        for d in (2, 1, 3):
            for s in range(2):
                peer = device((x + d) % NX, y, c, z) if s == 0 else device(x, (y + d) % NY, c, z)
                own = query[h].at[x, y, c, quarters[s]]
                line[h, s, d] = go(own, own, line_send.at[h, s, d], line_recv.at[h, s, d], peer)

    def to_core(h, index, block):
        share[h, index] = go(
            block,
            block,
            share_send.at[h, index],
            share_recv.at[h, index],
            device(x, y, 1 - c, z),
        )

    def send_cross(h):
        for s in range(2):
            for d in (1, 3, 2):
                line[h, s, d].wait_recv()
            block = (
                query[h].at[:, y, c, quarters[s]] if s == 0 else query[h].at[x, :, c, quarters[s]]
            )
            for d in (2, 1, 3):
                peer = device(x, (y + d) % NY, c, z) if s == 0 else device((x + d) % NX, y, c, z)
                cross[h, s, d] = go(
                    block, block, cross_send.at[h, s, d], cross_recv.at[h, s, d], peer
                )
            to_core(h, s * NX, block)

    def share_cross(h):
        for d in (1, 3, 2):
            for s in range(2):
                cross[h, s, d].wait_recv()
                if s == 0:
                    block = query[h].at[:, (y + NY - d) % NY, c, quarters[s]]
                else:
                    block = query[h].at[(x + NX - d) % NX, :, c, quarters[s]]
                to_core(h, s * NX + d, block)

    def wait_query(h):
        for index in range(2 * NX):
            share[h, index].wait_recv()

    loads[0].wait()
    loads[1].wait()
    project_query(0)
    pl.semaphore_wait(barrier, len(peers))
    send_line(0)
    project_query(1)
    send_line(1)
    gate_all[z] = silu(jnp.dot(normed[...], proj[0], preferred_element_type=F32)).astype(BF16)
    gates = []
    for d in HEADS_FAR_FIRST:
        own = gate_all.at[z]
        gates.append(
            go(own, own, gate_send.at[d], gate_recv.at[d], device(x, y, c, (z + d) % NZ))
        )
    for index in range(3, 6):
        loads[index].wait()
    sort_slots(user_row[...], block_row[...], length_row[...], table_rows)
    to_scalars = pltpu.make_async_copy(table_rows, table, load_sem.at[len(pairs)])
    to_scalars.start()
    send_cross(0)
    send_cross(1)
    for h in range(2):
        sums[h][SLOTS_HERE] = jnp.zeros((HALF, DH), BF16)
    total[...] = jnp.zeros((HALF, DH), F32)
    to_scalars.wait()
    loads[6].wait()
    share_cross(0)
    wait_query(0)

    core, peer_copies = {}, {}

    def chip_user(kx, ky, which):
        return (kx * NY + ky) * 2 + which

    def send_core(h):
        for dx in FAR_FIRST:
            kx = (x + dx) % NX
            for ky in range(NY):
                core_out[h, kx, ky] = sums[h][table[LAST, chip_user(kx, ky, 1 - c)]]
            core[h, dx] = go(
                core_out.at[h, kx],
                core_in.at[h, kx],
                core_send.at[h, dx],
                core_recv.at[h, dx],
                device(x, y, 1 - c, z),
            )

    def send_peers(h):
        for dx in FAR_FIRST:
            core[h, dx].wait_recv()
            kx = (x + dx) % NX
            for dy in FAR_FIRST:
                ky = (y + dy) % NY
                mine = sums[h][table[LAST, chip_user(kx, ky, c)]].astype(F32)
                offset = dx * NY + dy
                peer_out[h, offset] = (mine + core_in[h, kx, ky].astype(F32)).astype(BF16)
                if offset:
                    peer_copies[h, offset] = go(
                        peer_out.at[h, offset],
                        peer_in.at[h, offset],
                        peer_send.at[h, offset],
                        peer_recv.at[h, offset],
                        device(kx, ky, c, z),
                    )

    head = {}

    def send_heads(h):
        value = peer_out[h, 0].astype(F32)
        for offset in range(1, NX * NY):
            peer_copies[h, offset].wait_recv()
            value += peer_in[h, offset].astype(F32)
        attention[h, z] = value.astype(BF16)
        for d in HEADS_FAR_FIRST:
            own = attention.at[h, z]
            head[h, d] = go(
                own, own, head_send.at[h, d], head_recv.at[h, d], device(x, y, c, (z + d) % NZ)
            )

    def finish(h):
        for d in range(1, NZ):
            head[h, d].wait_recv()
        for part in range(2):
            rows = pl.ds(part * QUARTER, QUARTER)
            out_rows = pl.ds(h * HALF + part * QUARTER, QUARTER)
            whole = jnp.concatenate([attention[h, k, rows].astype(F32) for k in range(NZ)], axis=1)
            gate = jnp.concatenate([gate_all[k, out_rows].astype(F32) for k in range(NZ)], axis=1)
            gated = (layer_norm(whole, attention_gain[...]) * gate).astype(BF16)
            projected = jnp.dot(gated, weight[...], preferred_element_type=F32)
            cols = cand_rows[out_rows, pl.ds(pl.multiple_of(z * DH, DH), DH)].astype(F32)
            result[0, out_rows, :] = (cols + projected).astype(BF16)

    attend(table, query_a.reshape(USERS, HALF, DH), cache, sums_a, total, 0, ROUNDS - 1)
    share_cross(1)
    attend(table, query_a.reshape(USERS, HALF, DH), cache, sums_a, total, ROUNDS - 1, ROUNDS)
    send_core(0)
    wait_query(1)
    total[...] = jnp.zeros((HALF, DH), F32)
    attend(table, query_b.reshape(USERS, HALF, DH), cache, sums_b, total, 0, 1)
    send_peers(0)
    attend(table, query_b.reshape(USERS, HALF, DH), cache, sums_b, total, 1, ROUNDS)
    send_core(1)
    send_peers(1)
    send_heads(0)
    send_heads(1)
    loads[7].wait()
    loads[8].wait()
    for copy in gates:
        copy.wait_recv()
    finish(0)
    finish(1)
    for copy in sends:
        copy.wait_send()


def local(
    candidates,
    input_gain,
    proj_weight,
    history_cache,
    slot_user,
    slot_block,
    history_len,
    attention_gain,
    out_weight,
):
    dma = pltpu.SemaphoreType.DMA
    vmem = pltpu.VMEM
    operands = (
        candidates,
        input_gain.reshape(1, D),
        proj_weight,
        history_cache,
        slot_user.reshape(1, SLOTS_HERE),
        slot_block.reshape(1, SLOTS_HERE),
        history_len.reshape(1, USERS),
        attention_gain.reshape(1, D),
        out_weight,
    )
    return pl.pallas_call(
        kernel,
        out_shape=jax.ShapeDtypeStruct((1, CANDS, DH), BF16),
        in_specs=[pl.BlockSpec(memory_space=pl.ANY)] * len(operands),
        out_specs=pl.BlockSpec(memory_space=vmem),
        scratch_shapes=[
            vmem((CANDS, D), BF16),
            vmem((1, D), F32),
            vmem((2, D, DH), BF16),
            vmem((SLOTS_HERE, BLK, 2 * DH), BF16),
            vmem((1, SLOTS_HERE), I32),
            vmem((1, SLOTS_HERE), I32),
            vmem((1, USERS), I32),
            vmem((1, D), F32),
            vmem((D, DH), BF16),
            vmem((CANDS, D), BF16),
            vmem((NX, NY, 2, HALF, DH), BF16),
            vmem((NX, NY, 2, HALF, DH), BF16),
            vmem((NZ, CANDS, DH), BF16),
            vmem((8, 128), I32),
            pltpu.SMEM((8, 128), I32),
            vmem((SLOTS_HERE + 1, HALF, DH), BF16),
            vmem((SLOTS_HERE + 1, HALF, DH), BF16),
            vmem((HALF, DH), F32),
            vmem((2, NX, NY, HALF, DH), BF16),
            vmem((2, NX, NY, HALF, DH), BF16),
            vmem((2, NX * NY, HALF, DH), BF16),
            vmem((2, NX * NY, HALF, DH), BF16),
            vmem((2, NZ, HALF, DH), BF16),
            dma((len(operands) + 1,)),
            dma((2, 2, NX)),
            dma((2, 2, NX)),
            dma((2, 2, NX)),
            dma((2, 2, NX)),
            dma((2, 2 * NX)),
            dma((2, 2 * NX)),
            dma((NZ,)),
            dma((NZ,)),
            dma((2, NX)),
            dma((2, NX)),
            dma((2, NX * NY)),
            dma((2, NX * NY)),
            dma((2, NZ)),
            dma((2, NZ)),
        ],
        compiler_params=pltpu.CompilerParams(
            collective_id=0, has_side_effects=True, vmem_limit_bytes=48 << 20
        ),
        name="layer",
    )(*[pltpu.with_memory_space_constraint(operand, pltpu.HBM) for operand in operands])


def solution(mesh):
    return jax.shard_map(
        local,
        mesh=mesh,
        in_specs=(
            P("cand", None, None),
            P(),
            P(None, None, "hist"),
            P("cand", "hist", None, None),
            P("cand"),
            P("cand"),
            P(),
            P(),
            P(None, "hist"),
        ),
        out_specs=P("cand", None, "hist"),
        check_vma=False,
    )
```

```python
import functools

import jax
import jax.numpy as jnp
from jax import lax
from jax.experimental import pallas as pl
from jax.experimental.pallas import tpu as pltpu
from jax.sharding import PartitionSpec as P

D = 1024
DH = 128
CANDS = 256
HALF = CANDS // 2
QUARTER = CANDS // 4
BLK = 512
TILE = 256
SLOTS_HERE = 40
USERS = 32
NX, NY, NZ = 4, 4, 8
UNROLL = 4
ROUNDS = SLOTS_HERE // (2 * UNROLL)
F32 = jnp.float32
BF16 = jnp.bfloat16
I32 = jnp.int32
MESH = pl.DeviceIdType.MESH
HALF_SCALE = 0.5 * DH ** (-0.5)
FAR_FIRST = (2, 1, 3, 0)
HEADS_FAR_FIRST = (4, 3, 5, 2, 6, 1, 7)
SLOT, OWNER, COUNT, SAME, LAST = range(5)


def place():
    cand = lax.axis_index("cand")
    return cand // (2 * NY), (cand // 2) % NY, cand % 2, lax.axis_index("hist")


def device(x, y, c, z):
    return (z, (x * NY + y) * 2 + c)


def remote(src, dst, send_sem, recv_sem, peer):
    return pltpu.make_async_remote_copy(
        src_ref=src,
        dst_ref=dst,
        send_sem=send_sem,
        recv_sem=recv_sem,
        device_id=peer,
        device_id_type=MESH,
    )


def silu(value):
    half = 0.5 * value
    return half + half * jnp.tanh(half)


def layer_norm(rows, gain):
    centred = rows - jnp.mean(rows, axis=-1, keepdims=True)
    row_var = jnp.mean(centred * centred, axis=-1, keepdims=True)
    return centred * lax.rsqrt(row_var + 1e-05) * gain


def sort_slots(user_row, block_row, length_row, table):
    shape = (SLOTS_HERE, SLOTS_HERE)
    row_id = lax.broadcasted_iota(I32, shape, 0)
    col_id = lax.broadcasted_iota(I32, shape, 1)
    diagonal = row_id == col_id
    slot = lax.broadcasted_iota(I32, (SLOTS_HERE, 1), 0)
    user_id = lax.broadcasted_iota(I32, (SLOTS_HERE, USERS), 1)

    def across(mask, value):
        return jnp.sum(jnp.where(mask, value, 0), axis=1, keepdims=True)

    def down(mask, value):
        return jnp.sum(jnp.where(mask, value, 0), axis=0, keepdims=True)

    user = across(diagonal, user_row)
    block = across(diagonal, block_row)
    length = across(user_id == user, length_row)
    count = jnp.clip(length - block * BLK, 0, BLK)
    live = (block >= 0) & (count > 0)
    key = jnp.where(live, user * SLOTS_HERE, USERS * SLOTS_HERE) + slot
    key_row = down(diagonal, key)
    rank = across(key_row < key, 1)
    here = rank == col_id
    owner = down(here, user)
    before = down(rank + 1 == col_id, user + 1)
    through = down(live & (user <= user_id), 1)
    mine = down(live & (user == user_id), 1)
    table[...] = jnp.zeros_like(table)
    table[SLOT : SLOT + 1, :SLOTS_HERE] = down(here, slot)
    table[OWNER : OWNER + 1, :SLOTS_HERE] = owner
    table[COUNT : COUNT + 1, :SLOTS_HERE] = down(here, jnp.where(live, count, 0))
    table[SAME : SAME + 1, :SLOTS_HERE] = (before == owner + 1).astype(I32)
    table[LAST : LAST + 1, :USERS] = jnp.where(mine > 0, through - 1, SLOTS_HERE)


def attend(table, query, cache, sums, total, first, last):
    event = lax.broadcasted_iota(I32, (1, BLK), 1)
    blank = jnp.zeros((HALF, DH), BF16)

    def weigh(scores, scale):
        half = scores * scale
        return (half + half * jnp.tanh(half)).astype(BF16)

    def step(round_id, _):
        for turn in range(UNROLL):
            entry = (round_id * UNROLL + turn) * 2
            slot_a, slot_b = table[SLOT, entry], table[SLOT, entry + 1]
            scale_a = jnp.where(event < table[COUNT, entry], HALF_SCALE, 0.0)
            scale_b = jnp.where(event < table[COUNT, entry + 1], HALF_SCALE, 0.0)
            queries = jnp.concatenate(
                [
                    jnp.concatenate([query[table[OWNER, entry]], blank], axis=1),
                    jnp.concatenate([blank, query[table[OWNER, entry + 1]]], axis=1),
                ],
                axis=0,
            )
            value = jnp.zeros((2 * HALF, 2 * DH), F32)
            for tile in range(BLK // TILE):
                cols = slice(tile * TILE, (tile + 1) * TILE)
                keys = jnp.concatenate(
                    [cache[slot_a, cols, :DH], cache[slot_b, cols, :DH]], axis=1
                )
                values = jnp.concatenate(
                    [cache[slot_a, cols, DH:], cache[slot_b, cols, DH:]], axis=1
                )
                scores = lax.dot_general(
                    queries, keys, (((1,), (1,)), ((), ())), preferred_element_type=F32
                )
                weights = jnp.concatenate(
                    [weigh(scores[:HALF], scale_a[:, cols]), weigh(scores[HALF:], scale_b[:, cols])],
                    axis=0,
                )
                value += jnp.dot(weights, values, preferred_element_type=F32)
            run = total[...] * table[SAME, entry].astype(F32) + value[:HALF, :DH]
            sums[entry] = run.astype(BF16)
            run = run * table[SAME, entry + 1].astype(F32) + value[HALF:, DH:]
            sums[entry + 1] = run.astype(BF16)
            total[...] = run
        return 0

    lax.fori_loop(first, last, step, 0)


def kernel(
    cand_hbm,
    input_gain_hbm,
    proj_hbm,
    cache_hbm,
    user_hbm,
    block_hbm,
    length_hbm,
    attention_gain_hbm,
    weight_hbm,
    result,
    cand_rows,
    input_gain,
    proj,
    cache,
    user_row,
    block_row,
    length_row,
    attention_gain,
    weight,
    normed,
    query_a,
    query_b,
    gate_all,
    table_rows,
    table,
    sums_a,
    sums_b,
    total,
    core_out,
    core_in,
    peer_out,
    peer_in,
    attention,
    load_sem,
    line_recv,
    cross_recv,
    share_recv,
    gate_recv,
    core_recv,
    peer_recv,
    head_recv,
    send_sem,
):
    x, y, c, z = place()
    xs = [lax.rem(x + d, NX) for d in range(NX)]
    ys = [lax.rem(y + d, NY) for d in range(NY)]
    zs = [lax.rem(z + d, NZ) for d in range(NZ)]
    sibling = device(x, y, 1 - c, z)
    barrier = pltpu.get_barrier_semaphore()
    peers = [sibling]
    peers += [
        device(xs[dx], ys[dy], c, z) for dx in range(NX) for dy in range(NY) if dx or dy
    ]
    peers += [device(x, y, c, zs[d]) for d in range(1, NZ)]
    halves = (pl.ds(0, HALF), pl.ds(HALF, HALF))
    pairs = [
        (cand_hbm.at[0, halves[0]], cand_rows.at[halves[0]]),
        (input_gain_hbm, input_gain),
        (proj_hbm.at[1], proj.at[1]),
        (cand_hbm.at[0, halves[1]], cand_rows.at[halves[1]]),
        (proj_hbm.at[0], proj.at[0]),
        (user_hbm, user_row),
        (block_hbm, block_row),
        (length_hbm, length_row),
        (cache_hbm.at[:, 0], cache),
        (attention_gain_hbm, attention_gain),
        (weight_hbm, weight),
    ]
    loads = [
        pltpu.make_async_copy(src, dst, load_sem.at[i]) for i, (src, dst) in enumerate(pairs)
    ]
    for load in loads[:8]:
        load.start()
    for peer in peers:
        pl.semaphore_signal(barrier, inc=1, device_id=peer, device_id_type=MESH)

    query = (query_a, query_b)
    sums = (sums_a, sums_b)
    quarters = (pl.ds(0, QUARTER), pl.ds(QUARTER, QUARTER))
    LINE, CROSS, SHARE, CORE, PEER, HEAD = (0, 2, 4, 6, 8, 10)
    GATE = 12

    def go(src, dst, group, recv_sem, peer):
        remote(src, dst, send_sem.at[group], recv_sem, peer).start()

    def arrived(ref, recv_sem):
        remote(ref, ref, send_sem.at[0], recv_sem, sibling).wait_recv()

    def sent(ref, group):
        remote(ref, ref, send_sem.at[group], gate_recv.at[0], sibling).wait_send()

    def project_query(h):
        loads[3 * h].wait()
        for part in range(2):
            rows = pl.ds(h * HALF + part * QUARTER, QUARTER)
            normed[rows, :] = layer_norm(
                cand_rows[rows, :].astype(F32), input_gain[...]
            ).astype(BF16)
        if h == 0:
            loads[2].wait()
        query[h][x, y, c] = silu(
            jnp.dot(normed[halves[h], :], proj[1], preferred_element_type=F32)
        ).astype(BF16)

    def send_line(h):
        for d in (2, 1, 3):
            for s in range(2):
                peer = device(xs[d], y, c, z) if s == 0 else device(x, ys[d], c, z)
                own = query[h].at[x, y, c, quarters[s]]
                go(own, own, LINE + h, line_recv.at[h, s], peer)

    def to_core(h, block):
        go(block, block, SHARE + h, share_recv.at[h], sibling)

    def send_cross(h):
        for s in range(2):
            arrived(query[h].at[pl.ds(0, NX - 1), 0, 0, quarters[s]], line_recv.at[h, s])
            block = (
                query[h].at[:, y, c, quarters[s]] if s == 0 else query[h].at[x, :, c, quarters[s]]
            )
            for d in (2, 1, 3):
                peer = device(x, ys[d], c, z) if s == 0 else device(xs[d], y, c, z)
                go(block, block, CROSS + h, cross_recv.at[h, s, d - 1], peer)
            to_core(h, block)

    def share_cross(h):
        for d in (1, 3, 2):
            for s in range(2):
                if s == 0:
                    block = query[h].at[:, ys[NY - d], c, quarters[s]]
                else:
                    block = query[h].at[xs[NX - d], :, c, quarters[s]]
                arrived(block, cross_recv.at[h, s, d - 1])
                to_core(h, block)

    def wait_query(h):
        arrived(query[h].at[:, :, 0], share_recv.at[h])

    loads[1].wait()
    project_query(0)
    pl.semaphore_wait(barrier, len(peers))
    send_line(0)
    project_query(1)
    send_line(1)
    loads[4].wait()
    gate_all[z] = silu(jnp.dot(normed[...], proj[0], preferred_element_type=F32)).astype(BF16)
    for d in HEADS_FAR_FIRST:
        own = gate_all.at[z]
        go(own, own, GATE, gate_recv.at[0], device(x, y, c, zs[d]))
    for load in loads[8:]:
        load.start()
    for load in loads[5:8]:
        load.wait()
    sort_slots(user_row[...], block_row[...], length_row[...], table_rows)
    to_scalars = pltpu.make_async_copy(table_rows, table, load_sem.at[len(pairs)])
    to_scalars.start()
    send_cross(0)
    send_cross(1)
    for h in range(2):
        sums[h][SLOTS_HERE] = jnp.zeros((HALF, DH), BF16)
    total[...] = jnp.zeros((HALF, DH), F32)
    to_scalars.wait()
    loads[8].wait()
    share_cross(0)
    wait_query(0)

    def chip_user(kx, ky, which):
        return (kx * NY + ky) * 2 + which

    def send_core(h):
        for dx in FAR_FIRST:
            kx = xs[dx]
            for ky in range(NY):
                core_out[h, kx, ky] = sums[h][table[LAST, chip_user(kx, ky, 1 - c)]]
            go(core_out.at[h, kx], core_in.at[h, kx], CORE + h, core_recv.at[h, dx], sibling)

    def send_peers(h, p, first):
        for dx in FAR_FIRST:
            kx = xs[dx]
            if first:
                arrived(core_in.at[h, kx], core_recv.at[h, dx])
            for dy in FAR_FIRST:
                mine = sums[h][table[LAST, chip_user(kx, ys[dy], c)], quarters[p]]
                peer_out[h, dx * NY + dy, quarters[p]] = mine + core_in[h, kx, ys[dy], quarters[p]]
            for dy in FAR_FIRST:
                offset = dx * NY + dy
                if offset:
                    go(
                        peer_out.at[h, offset, quarters[p]],
                        peer_in.at[h, offset, quarters[p]],
                        PEER + h,
                        peer_recv.at[h, p],
                        device(kx, ys[dy], c, z),
                    )

    def send_heads(h, p):
        others = pl.ds(1, NX * NY - 1)
        arrived(peer_in.at[h, others, quarters[p]], peer_recv.at[h, p])
        value = peer_out[h, 0, quarters[p]].astype(F32)
        for offset in range(1, NX * NY):
            value += peer_in[h, offset, quarters[p]].astype(F32)
        attention[h, z, quarters[p]] = value.astype(BF16)
        own = attention.at[h, z, quarters[p]]
        for d in HEADS_FAR_FIRST:
            go(own, own, HEAD + h, head_recv.at[h, p], device(x, y, c, zs[d]))

    def finish(h, p):
        arrived(attention.at[h, pl.ds(0, NZ - 1), quarters[p]], head_recv.at[h, p])
        out_rows = pl.ds(h * HALF + p * QUARTER, QUARTER)
        whole = jnp.concatenate(
            [attention[h, k, quarters[p]].astype(F32) for k in range(NZ)], axis=1
        )
        gate = jnp.concatenate([gate_all[k, out_rows].astype(F32) for k in range(NZ)], axis=1)
        gated = (layer_norm(whole, attention_gain[...]) * gate).astype(BF16)
        projected = jnp.dot(gated, weight[...], preferred_element_type=F32)
        cols = cand_rows[out_rows, pl.ds(pl.multiple_of(z * DH, DH), DH)].astype(F32)
        result[0, out_rows, :] = (cols + projected).astype(BF16)

    flat_a = query_a.reshape(USERS, HALF, DH)
    flat_b = query_b.reshape(USERS, HALF, DH)
    attend(table, flat_a, cache, sums_a, total, 0, 3)
    share_cross(1)
    attend(table, flat_a, cache, sums_a, total, 3, ROUNDS)
    send_core(0)
    wait_query(1)
    total[...] = jnp.zeros((HALF, DH), F32)
    attend(table, flat_b, cache, sums_b, total, 0, 1)
    send_peers(0, 0, True)
    attend(table, flat_b, cache, sums_b, total, 1, 2)
    send_peers(0, 1, False)
    attend(table, flat_b, cache, sums_b, total, 2, ROUNDS)
    send_core(1)
    send_heads(0, 0)
    send_peers(1, 0, True)
    send_peers(1, 1, False)
    send_heads(0, 1)
    send_heads(1, 0)
    loads[9].wait()
    loads[10].wait()
    arrived(gate_all.at[pl.ds(0, NZ - 1)], gate_recv.at[0])
    finish(0, 0)
    finish(0, 1)
    send_heads(1, 1)
    finish(1, 0)
    finish(1, 1)
    for h in range(2):
        sent(query[h].at[pl.ds(0, NX - 1), 0, 0], LINE + h)
        sent(query[h].at[pl.ds(0, NX - 1), :, 0], CROSS + h)
        sent(query[h].at[:, :, 0], SHARE + h)
        sent(core_out.at[h], CORE + h)
        sent(peer_out.at[h, pl.ds(1, NX * NY - 1)], PEER + h)
        sent(attention.at[h, pl.ds(0, NZ - 1)], HEAD + h)
    sent(gate_all.at[pl.ds(0, NZ - 1)], GATE)


def local(
    candidates,
    input_gain,
    proj_weight,
    history_cache,
    slot_user,
    slot_block,
    history_len,
    attention_gain,
    out_weight,
):
    dma = pltpu.SemaphoreType.DMA
    vmem = pltpu.VMEM
    operands = (
        candidates,
        input_gain.reshape(1, D),
        proj_weight,
        history_cache,
        slot_user.reshape(1, SLOTS_HERE),
        slot_block.reshape(1, SLOTS_HERE),
        history_len.reshape(1, USERS),
        attention_gain.reshape(1, D),
        out_weight,
    )
    return pl.pallas_call(
        kernel,
        out_shape=jax.ShapeDtypeStruct((1, CANDS, DH), BF16),
        in_specs=[pl.BlockSpec(memory_space=pl.ANY)] * len(operands),
        out_specs=pl.BlockSpec(memory_space=vmem),
        scratch_shapes=[
            vmem((CANDS, D), BF16),
            vmem((1, D), F32),
            vmem((2, D, DH), BF16),
            vmem((SLOTS_HERE, BLK, 2 * DH), BF16),
            vmem((1, SLOTS_HERE), I32),
            vmem((1, SLOTS_HERE), I32),
            vmem((1, USERS), I32),
            vmem((1, D), F32),
            vmem((D, DH), BF16),
            vmem((CANDS, D), BF16),
            vmem((NX, NY, 2, HALF, DH), BF16),
            vmem((NX, NY, 2, HALF, DH), BF16),
            vmem((NZ, CANDS, DH), BF16),
            vmem((8, 128), I32),
            pltpu.SMEM((8, 128), I32),
            vmem((SLOTS_HERE + 1, HALF, DH), BF16),
            vmem((SLOTS_HERE + 1, HALF, DH), BF16),
            vmem((HALF, DH), F32),
            vmem((2, NX, NY, HALF, DH), BF16),
            vmem((2, NX, NY, HALF, DH), BF16),
            vmem((2, NX * NY, HALF, DH), BF16),
            vmem((2, NX * NY, HALF, DH), BF16),
            vmem((2, NZ, HALF, DH), BF16),
            dma((len(operands) + 3,)),
            dma((2, 2)),
            dma((2, 2, NX - 1)),
            dma((2,)),
            dma((1,)),
            dma((2, NX)),
            dma((2, 2)),
            dma((2, 2)),
            dma((13,)),
        ],
        compiler_params=pltpu.CompilerParams(
            collective_id=0, has_side_effects=True, vmem_limit_bytes=48 << 20
        ),
        name="layer",
    )(*[pltpu.with_memory_space_constraint(operand, pltpu.HBM) for operand in operands])


def solution(mesh):
    return jax.shard_map(
        local,
        mesh=mesh,
        in_specs=(
            P("cand", None, None),
            P(),
            P(None, None, "hist"),
            P("cand", "hist", None, None),
            P("cand"),
            P("cand"),
            P(),
            P(),
            P(None, "hist"),
        ),
        out_specs=P("cand", None, "hist"),
        check_vma=False,
    )
```

```python
import functools

import jax
import jax.numpy as jnp
from jax import lax
from jax.experimental import pallas as pl
from jax.experimental.pallas import tpu as pltpu
from jax.sharding import PartitionSpec as P

D = 1024
DH = 128
CANDS = 256
HALF = CANDS // 2
QUARTER = CANDS // 4
BLK = 512
TILE = 256
SLOTS_HERE = 40
USERS = 32
NX, NY, NZ = 4, 4, 8
UNROLL = 4
ROUNDS = SLOTS_HERE // (2 * UNROLL)
F32 = jnp.float32
BF16 = jnp.bfloat16
I32 = jnp.int32
MESH = pl.DeviceIdType.MESH
HALF_SCALE = 0.5 * DH ** (-0.5)
FAR_FIRST = (2, 1, 3, 0)
PARTS = (2, 4)
HEADS_FAR_FIRST = (4, 3, 5, 2, 6, 1, 7)
SLOT, OWNER, COUNT, SAME, LAST = range(5)


def place():
    cand = lax.axis_index("cand")
    return cand // (2 * NY), (cand // 2) % NY, cand % 2, lax.axis_index("hist")


def device(x, y, c, z):
    return (z, (x * NY + y) * 2 + c)


def remote(src, dst, send_sem, recv_sem, peer):
    return pltpu.make_async_remote_copy(
        src_ref=src,
        dst_ref=dst,
        send_sem=send_sem,
        recv_sem=recv_sem,
        device_id=peer,
        device_id_type=MESH,
    )


def silu(value):
    half = 0.5 * value
    return half + half * jnp.tanh(half)


def layer_norm(rows, gain):
    centred = rows - jnp.mean(rows, axis=-1, keepdims=True)
    row_var = jnp.mean(centred * centred, axis=-1, keepdims=True)
    return centred * lax.rsqrt(row_var + 1e-05) * gain


def sort_slots(user_row, block_row, length_row, table):
    shape = (SLOTS_HERE, SLOTS_HERE)
    row_id = lax.broadcasted_iota(I32, shape, 0)
    col_id = lax.broadcasted_iota(I32, shape, 1)
    diagonal = row_id == col_id
    slot = lax.broadcasted_iota(I32, (SLOTS_HERE, 1), 0)
    user_id = lax.broadcasted_iota(I32, (SLOTS_HERE, USERS), 1)

    def across(mask, value):
        return jnp.sum(jnp.where(mask, value, 0), axis=1, keepdims=True)

    def down(mask, value):
        return jnp.sum(jnp.where(mask, value, 0), axis=0, keepdims=True)

    user = across(diagonal, user_row)
    block = across(diagonal, block_row)
    length = across(user_id == user, length_row)
    count = jnp.clip(length - block * BLK, 0, BLK)
    live = (block >= 0) & (count > 0)
    key = jnp.where(live, user * SLOTS_HERE, USERS * SLOTS_HERE) + slot
    key_row = down(diagonal, key)
    rank = across(key_row < key, 1)
    here = rank == col_id
    owner = down(here, user)
    before = down(rank + 1 == col_id, user + 1)
    through = down(live & (user <= user_id), 1)
    mine = down(live & (user == user_id), 1)
    table[...] = jnp.zeros_like(table)
    table[SLOT : SLOT + 1, :SLOTS_HERE] = down(here, slot)
    table[OWNER : OWNER + 1, :SLOTS_HERE] = owner
    table[COUNT : COUNT + 1, :SLOTS_HERE] = down(here, jnp.where(live, count, 0))
    table[SAME : SAME + 1, :SLOTS_HERE] = (before == owner + 1).astype(I32)
    table[LAST : LAST + 1, :USERS] = jnp.where(mine > 0, through - 1, SLOTS_HERE)


def attend(table, query, cache, sums, total, first, last):
    event = lax.broadcasted_iota(I32, (1, BLK), 1)
    blank = jnp.zeros((HALF, DH), BF16)

    def weigh(scores, scale):
        half = scores * scale
        return (half + half * jnp.tanh(half)).astype(BF16)

    def step(round_id, _):
        for turn in range(UNROLL):
            entry = (round_id * UNROLL + turn) * 2
            slot_a, slot_b = table[SLOT, entry], table[SLOT, entry + 1]
            scale_a = jnp.where(event < table[COUNT, entry], HALF_SCALE, 0.0)
            scale_b = jnp.where(event < table[COUNT, entry + 1], HALF_SCALE, 0.0)
            queries = jnp.concatenate(
                [
                    jnp.concatenate([query[table[OWNER, entry]], blank], axis=1),
                    jnp.concatenate([blank, query[table[OWNER, entry + 1]]], axis=1),
                ],
                axis=0,
            )
            value = jnp.zeros((2 * HALF, 2 * DH), F32)
            for tile in range(BLK // TILE):
                cols = slice(tile * TILE, (tile + 1) * TILE)
                keys = jnp.concatenate(
                    [cache[slot_a, cols, :DH], cache[slot_b, cols, :DH]], axis=1
                )
                values = jnp.concatenate(
                    [cache[slot_a, cols, DH:], cache[slot_b, cols, DH:]], axis=1
                )
                scores = lax.dot_general(
                    queries, keys, (((1,), (1,)), ((), ())), preferred_element_type=F32
                )
                weights = jnp.concatenate(
                    [weigh(scores[:HALF], scale_a[:, cols]), weigh(scores[HALF:], scale_b[:, cols])],
                    axis=0,
                )
                value += jnp.dot(weights, values, preferred_element_type=F32)
            run = total[...] * table[SAME, entry].astype(F32) + value[:HALF, :DH]
            sums[entry] = run.astype(BF16)
            run = run * table[SAME, entry + 1].astype(F32) + value[HALF:, DH:]
            sums[entry + 1] = run.astype(BF16)
            total[...] = run
        return 0

    lax.fori_loop(first, last, step, 0)


def kernel(
    cand_hbm,
    input_gain_hbm,
    proj_hbm,
    cache_hbm,
    user_hbm,
    block_hbm,
    length_hbm,
    attention_gain_hbm,
    weight_hbm,
    result,
    cand_rows,
    input_gain,
    proj,
    cache,
    user_row,
    block_row,
    length_row,
    attention_gain,
    weight,
    normed,
    query_a,
    query_b,
    gate_all,
    table_rows,
    table,
    sums_a,
    sums_b,
    total,
    core_out,
    core_in,
    peer_out,
    peer_in,
    attention,
    load_sem,
    line_recv,
    cross_recv,
    share_recv,
    gate_recv,
    core_recv,
    peer_recv,
    head_recv,
    send_sem,
):
    x, y, c, z = place()
    xs = [lax.rem(x + d, NX) for d in range(NX)]
    ys = [lax.rem(y + d, NY) for d in range(NY)]
    zs = [lax.rem(z + d, NZ) for d in range(NZ)]
    sibling = device(x, y, 1 - c, z)
    barrier = pltpu.get_barrier_semaphore()
    peers = [sibling]
    peers += [
        device(xs[dx], ys[dy], c, z) for dx in range(NX) for dy in range(NY) if dx or dy
    ]
    peers += [device(x, y, c, zs[d]) for d in range(1, NZ)]
    halves = (pl.ds(0, HALF), pl.ds(HALF, HALF))
    pairs = [
        (cand_hbm.at[0, halves[0]], cand_rows.at[halves[0]]),
        (input_gain_hbm, input_gain),
        (proj_hbm.at[1], proj.at[1]),
        (cand_hbm.at[0, halves[1]], cand_rows.at[halves[1]]),
        (proj_hbm.at[0], proj.at[0]),
        (user_hbm, user_row),
        (block_hbm, block_row),
        (length_hbm, length_row),
        (cache_hbm.at[:, 0], cache),
        (attention_gain_hbm, attention_gain),
        (weight_hbm, weight),
    ]
    loads = [
        pltpu.make_async_copy(src, dst, load_sem.at[i]) for i, (src, dst) in enumerate(pairs)
    ]
    for load in loads[:8]:
        load.start()
    for peer in peers:
        pl.semaphore_signal(barrier, inc=1, device_id=peer, device_id_type=MESH)

    query = (query_a, query_b)
    sums = (sums_a, sums_b)
    quarters = (pl.ds(0, QUARTER), pl.ds(QUARTER, QUARTER))
    LINE, CROSS, SHARE, CORE, PEER, HEAD = (0, 2, 4, 6, 8, 10)
    GATE = 12

    def go(src, dst, group, recv_sem, peer):
        remote(src, dst, send_sem.at[group], recv_sem, peer).start()

    def arrived(ref, recv_sem):
        remote(ref, ref, send_sem.at[0], recv_sem, sibling).wait_recv()

    def sent(ref, group):
        remote(ref, ref, send_sem.at[group], gate_recv.at[0], sibling).wait_send()

    def project_query(h):
        loads[3 * h].wait()
        for part in range(2):
            rows = pl.ds(h * HALF + part * QUARTER, QUARTER)
            normed[rows, :] = layer_norm(
                cand_rows[rows, :].astype(F32), input_gain[...]
            ).astype(BF16)
        if h == 0:
            loads[2].wait()
        query[h][x, y, c] = silu(
            jnp.dot(normed[halves[h], :], proj[1], preferred_element_type=F32)
        ).astype(BF16)

    def send_line(h):
        for d in (2, 1, 3):
            for s in range(2):
                peer = device(xs[d], y, c, z) if s == 0 else device(x, ys[d], c, z)
                own = query[h].at[x, y, c, quarters[s]]
                go(own, own, LINE + h, line_recv.at[h, s], peer)

    def to_core(h, block):
        go(block, block, SHARE + h, share_recv.at[h], sibling)

    def send_cross(h):
        for s in range(2):
            arrived(query[h].at[pl.ds(0, NX - 1), 0, 0, quarters[s]], line_recv.at[h, s])
            block = (
                query[h].at[:, y, c, quarters[s]] if s == 0 else query[h].at[x, :, c, quarters[s]]
            )
            for d in (2, 1, 3):
                peer = device(x, ys[d], c, z) if s == 0 else device(xs[d], y, c, z)
                go(block, block, CROSS + h, cross_recv.at[h, s, d - 1], peer)
            to_core(h, block)

    def share_cross(h):
        for d in (1, 3, 2):
            for s in range(2):
                if s == 0:
                    block = query[h].at[:, ys[NY - d], c, quarters[s]]
                else:
                    block = query[h].at[xs[NX - d], :, c, quarters[s]]
                arrived(block, cross_recv.at[h, s, d - 1])
                to_core(h, block)

    def wait_query(h):
        arrived(query[h].at[:, :, 0], share_recv.at[h])

    loads[1].wait()
    project_query(0)
    pl.semaphore_wait(barrier, len(peers))
    send_line(0)
    project_query(1)
    send_line(1)
    loads[4].wait()
    gate_all[z] = silu(jnp.dot(normed[...], proj[0], preferred_element_type=F32)).astype(BF16)
    for d in HEADS_FAR_FIRST:
        own = gate_all.at[z]
        go(own, own, GATE, gate_recv.at[0], device(x, y, c, zs[d]))
    for load in loads[8:]:
        load.start()
    for load in loads[5:8]:
        load.wait()
    sort_slots(user_row[...], block_row[...], length_row[...], table_rows)
    to_scalars = pltpu.make_async_copy(table_rows, table, load_sem.at[len(pairs)])
    to_scalars.start()
    send_cross(0)
    for h in range(2):
        sums[h][SLOTS_HERE] = jnp.zeros((HALF, DH), BF16)
    total[...] = jnp.zeros((HALF, DH), F32)
    to_scalars.wait()
    loads[8].wait()
    share_cross(0)
    send_cross(1)
    wait_query(0)

    def chip_user(kx, ky, which):
        return (kx * NY + ky) * 2 + which

    def part(h, p):
        size = HALF // PARTS[h]
        return pl.ds(p * size, size)

    def send_core(h, p):
        rows = part(h, p)
        for kx in range(NX):
            for ky in range(NY):
                user = chip_user(kx, ky, 1 - c)
                core_out[h, kx, ky, rows] = sums[h][table[LAST, user], rows]
        go(
            core_out.at[h, :, :, rows],
            core_in.at[h, :, :, rows],
            CORE + h,
            core_recv.at[h, p],
            sibling,
        )

    def send_peers(h, p):
        rows = part(h, p)
        arrived(core_in.at[h, :, :, rows], core_recv.at[h, p])
        for dx in FAR_FIRST:
            kx = xs[dx]
            for dy in FAR_FIRST:
                mine = sums[h][table[LAST, chip_user(kx, ys[dy], c)], rows]
                peer_out[h, dx * NY + dy, rows] = mine + core_in[h, kx, ys[dy], rows]
            for dy in FAR_FIRST:
                offset = dx * NY + dy
                if offset:
                    go(
                        peer_out.at[h, offset, rows],
                        peer_in.at[h, offset, rows],
                        PEER + h,
                        peer_recv.at[h, p],
                        device(kx, ys[dy], c, z),
                    )

    def send_heads(h, p):
        rows = part(h, p)
        arrived(peer_in.at[h, pl.ds(1, NX * NY - 1), rows], peer_recv.at[h, p])
        value = peer_out[h, 0, rows].astype(F32)
        for offset in range(1, NX * NY):
            value += peer_in[h, offset, rows].astype(F32)
        attention[h, z, rows] = value.astype(BF16)
        own = attention.at[h, z, rows]
        for d in HEADS_FAR_FIRST:
            go(own, own, HEAD + h, head_recv.at[h, p], device(x, y, c, zs[d]))

    def finish(h, p):
        rows = part(h, p)
        arrived(attention.at[h, pl.ds(0, NZ - 1), rows], head_recv.at[h, p])
        out_rows = pl.ds(h * HALF + rows.start, rows.size)
        whole = jnp.concatenate([attention[h, k, rows].astype(F32) for k in range(NZ)], axis=1)
        gate = jnp.concatenate([gate_all[k, out_rows].astype(F32) for k in range(NZ)], axis=1)
        gated = (layer_norm(whole, attention_gain[...]) * gate).astype(BF16)
        projected = jnp.dot(gated, weight[...], preferred_element_type=F32)
        cols = cand_rows[out_rows, pl.ds(pl.multiple_of(z * DH, DH), DH)].astype(F32)
        result[0, out_rows, :] = (cols + projected).astype(BF16)

    flat_a = query_a.reshape(USERS, HALF, DH)
    flat_b = query_b.reshape(USERS, HALF, DH)
    attend(table, flat_a, cache, sums_a, total, 0, 3)
    share_cross(1)
    attend(table, flat_a, cache, sums_a, total, 3, ROUNDS)
    send_core(0, 0)
    send_core(0, 1)
    wait_query(1)
    total[...] = jnp.zeros((HALF, DH), F32)
    attend(table, flat_b, cache, sums_b, total, 0, 1)
    send_peers(0, 0)
    attend(table, flat_b, cache, sums_b, total, 1, 2)
    send_peers(0, 1)
    attend(table, flat_b, cache, sums_b, total, 2, ROUNDS)
    for p in range(PARTS[1]):
        send_core(1, p)
    send_heads(0, 0)
    send_peers(1, 0)
    send_peers(1, 1)
    send_heads(0, 1)
    send_peers(1, 2)
    send_peers(1, 3)
    loads[9].wait()
    loads[10].wait()
    arrived(gate_all.at[pl.ds(0, NZ - 1)], gate_recv.at[0])
    finish(0, 0)
    send_heads(1, 0)
    send_heads(1, 1)
    send_heads(1, 2)
    finish(0, 1)
    send_heads(1, 3)
    for p in range(PARTS[1]):
        finish(1, p)
    for h in range(2):
        sent(query[h].at[pl.ds(0, NX - 1), 0, 0], LINE + h)
        sent(query[h].at[pl.ds(0, NX - 1), :, 0], CROSS + h)
        sent(query[h].at[:, :, 0], SHARE + h)
        sent(core_out.at[h], CORE + h)
        sent(peer_out.at[h, pl.ds(1, NX * NY - 1)], PEER + h)
        sent(attention.at[h, pl.ds(0, NZ - 1)], HEAD + h)
    sent(gate_all.at[pl.ds(0, NZ - 1)], GATE)


def local(
    candidates,
    input_gain,
    proj_weight,
    history_cache,
    slot_user,
    slot_block,
    history_len,
    attention_gain,
    out_weight,
):
    dma = pltpu.SemaphoreType.DMA
    vmem = pltpu.VMEM
    operands = (
        candidates,
        input_gain.reshape(1, D),
        proj_weight,
        history_cache,
        slot_user.reshape(1, SLOTS_HERE),
        slot_block.reshape(1, SLOTS_HERE),
        history_len.reshape(1, USERS),
        attention_gain.reshape(1, D),
        out_weight,
    )
    return pl.pallas_call(
        kernel,
        out_shape=jax.ShapeDtypeStruct((1, CANDS, DH), BF16),
        in_specs=[pl.BlockSpec(memory_space=pl.ANY)] * len(operands),
        out_specs=pl.BlockSpec(memory_space=vmem),
        scratch_shapes=[
            vmem((CANDS, D), BF16),
            vmem((1, D), F32),
            vmem((2, D, DH), BF16),
            vmem((SLOTS_HERE, BLK, 2 * DH), BF16),
            vmem((1, SLOTS_HERE), I32),
            vmem((1, SLOTS_HERE), I32),
            vmem((1, USERS), I32),
            vmem((1, D), F32),
            vmem((D, DH), BF16),
            vmem((CANDS, D), BF16),
            vmem((NX, NY, 2, HALF, DH), BF16),
            vmem((NX, NY, 2, HALF, DH), BF16),
            vmem((NZ, CANDS, DH), BF16),
            vmem((8, 128), I32),
            pltpu.SMEM((8, 128), I32),
            vmem((SLOTS_HERE + 1, HALF, DH), BF16),
            vmem((SLOTS_HERE + 1, HALF, DH), BF16),
            vmem((HALF, DH), F32),
            vmem((2, NX, NY, HALF, DH), BF16),
            vmem((2, NX, NY, HALF, DH), BF16),
            vmem((2, NX * NY, HALF, DH), BF16),
            vmem((2, NX * NY, HALF, DH), BF16),
            vmem((2, NZ, HALF, DH), BF16),
            dma((len(operands) + 3,)),
            dma((2, 2)),
            dma((2, 2, NX - 1)),
            dma((2,)),
            dma((1,)),
            dma((2, 4)),
            dma((2, 4)),
            dma((2, 4)),
            dma((13,)),
        ],
        compiler_params=pltpu.CompilerParams(
            collective_id=0, has_side_effects=True, vmem_limit_bytes=48 << 20
        ),
        name="layer",
    )(*[pltpu.with_memory_space_constraint(operand, pltpu.HBM) for operand in operands])


def solution(mesh):
    return jax.shard_map(
        local,
        mesh=mesh,
        in_specs=(
            P("cand", None, None),
            P(),
            P(None, None, "hist"),
            P("cand", "hist", None, None),
            P("cand"),
            P("cand"),
            P(),
            P(),
            P(None, "hist"),
        ),
        out_specs=P("cand", None, "hist"),
        check_vma=False,
    )
```

```python
import functools

import jax
import jax.numpy as jnp
from jax import lax
from jax.experimental import pallas as pl
from jax.experimental.pallas import tpu as pltpu
from jax.sharding import PartitionSpec as P

D = 1024
DH = 128
CANDS = 256
HALF = CANDS // 2
QUARTER = CANDS // 4
BLK = 512
TILE = 256
SLOTS_HERE = 40
USERS = 32
NX, NY, NZ = 4, 4, 8
UNROLL = 4
ROUNDS = SLOTS_HERE // (2 * UNROLL)
F32 = jnp.float32
BF16 = jnp.bfloat16
I32 = jnp.int32
MESH = pl.DeviceIdType.MESH
HALF_SCALE = 0.5 * DH ** (-0.5)
FAR_FIRST = (2, 1, 3, 0)
PARTS = (2, 4)
HEADS_FAR_FIRST = (4, 3, 5, 2, 6, 1, 7)
SLOT, OWNER, COUNT, SAME, LAST = range(5)


def place():
    cand = lax.axis_index("cand")
    return cand // (2 * NY), (cand // 2) % NY, cand % 2, lax.axis_index("hist")


def device(x, y, c, z):
    return (z, (x * NY + y) * 2 + c)


def remote(src, dst, send_sem, recv_sem, peer):
    return pltpu.make_async_remote_copy(
        src_ref=src,
        dst_ref=dst,
        send_sem=send_sem,
        recv_sem=recv_sem,
        device_id=peer,
        device_id_type=MESH,
    )


def silu(value):
    half = 0.5 * value
    return half + half * jnp.tanh(half)


def layer_norm(rows, gain):
    centred = rows - jnp.mean(rows, axis=-1, keepdims=True)
    row_var = jnp.mean(centred * centred, axis=-1, keepdims=True)
    return centred * lax.rsqrt(row_var + 1e-05) * gain


def sort_slots(user_row, block_row, length_row, table):
    shape = (SLOTS_HERE, SLOTS_HERE)
    row_id = lax.broadcasted_iota(I32, shape, 0)
    col_id = lax.broadcasted_iota(I32, shape, 1)
    diagonal = row_id == col_id
    slot = lax.broadcasted_iota(I32, (SLOTS_HERE, 1), 0)
    user_id = lax.broadcasted_iota(I32, (SLOTS_HERE, USERS), 1)

    def across(mask, value):
        return jnp.sum(jnp.where(mask, value, 0), axis=1, keepdims=True)

    def down(mask, value):
        return jnp.sum(jnp.where(mask, value, 0), axis=0, keepdims=True)

    user = across(diagonal, user_row)
    block = across(diagonal, block_row)
    length = across(user_id == user, length_row)
    count = jnp.clip(length - block * BLK, 0, BLK)
    live = (block >= 0) & (count > 0)
    key = jnp.where(live, user * SLOTS_HERE, USERS * SLOTS_HERE) + slot
    key_row = down(diagonal, key)
    rank = across(key_row < key, 1)
    here = rank == col_id
    owner = down(here, user)
    before = down(rank + 1 == col_id, user + 1)
    through = down(live & (user <= user_id), 1)
    mine = down(live & (user == user_id), 1)
    table[...] = jnp.zeros_like(table)
    table[SLOT : SLOT + 1, :SLOTS_HERE] = down(here, slot)
    table[OWNER : OWNER + 1, :SLOTS_HERE] = owner
    table[COUNT : COUNT + 1, :SLOTS_HERE] = down(here, jnp.where(live, count, 0))
    table[SAME : SAME + 1, :SLOTS_HERE] = (before == owner + 1).astype(I32)
    table[LAST : LAST + 1, :USERS] = jnp.where(mine > 0, through - 1, SLOTS_HERE)


def attend(table, query, cache, sums, total, first, last):
    event = lax.broadcasted_iota(I32, (1, BLK), 1)
    blank = jnp.zeros((HALF, DH), BF16)

    def weigh(scores, scale):
        half = scores * scale
        return (half + half * jnp.tanh(half)).astype(BF16)

    def step(round_id, _):
        for turn in range(UNROLL):
            entry = (round_id * UNROLL + turn) * 2
            slot_a, slot_b = table[SLOT, entry], table[SLOT, entry + 1]
            scale_a = jnp.where(event < table[COUNT, entry], HALF_SCALE, 0.0)
            scale_b = jnp.where(event < table[COUNT, entry + 1], HALF_SCALE, 0.0)
            queries = jnp.concatenate(
                [
                    jnp.concatenate([query[table[OWNER, entry]], blank], axis=1),
                    jnp.concatenate([blank, query[table[OWNER, entry + 1]]], axis=1),
                ],
                axis=0,
            )
            value = jnp.zeros((2 * HALF, 2 * DH), F32)
            for tile in range(BLK // TILE):
                cols = slice(tile * TILE, (tile + 1) * TILE)
                keys = jnp.concatenate(
                    [cache[slot_a, cols, :DH], cache[slot_b, cols, :DH]], axis=1
                )
                values = jnp.concatenate(
                    [cache[slot_a, cols, DH:], cache[slot_b, cols, DH:]], axis=1
                )
                scores = lax.dot_general(
                    queries, keys, (((1,), (1,)), ((), ())), preferred_element_type=F32
                )
                weights = jnp.concatenate(
                    [weigh(scores[:HALF], scale_a[:, cols]), weigh(scores[HALF:], scale_b[:, cols])],
                    axis=0,
                )
                value += jnp.dot(weights, values, preferred_element_type=F32)
            run = total[...] * table[SAME, entry].astype(F32) + value[:HALF, :DH]
            sums[entry] = run.astype(BF16)
            run = run * table[SAME, entry + 1].astype(F32) + value[HALF:, DH:]
            sums[entry + 1] = run.astype(BF16)
            total[...] = run
        return 0

    lax.fori_loop(first, last, step, 0)


def kernel(
    cand_hbm,
    input_gain_hbm,
    proj_hbm,
    cache_hbm,
    user_hbm,
    block_hbm,
    length_hbm,
    attention_gain_hbm,
    weight_hbm,
    result,
    cand_rows,
    input_gain,
    proj,
    cache,
    user_row,
    block_row,
    length_row,
    attention_gain,
    weight,
    normed,
    query_a,
    query_b,
    gate_all,
    table_rows,
    table,
    sums_a,
    sums_b,
    total,
    core_out,
    core_in,
    peer_out,
    peer_in,
    attention,
    load_sem,
    line_recv,
    cross_recv,
    share_recv,
    gate_recv,
    core_recv,
    peer_recv,
    head_recv,
    send_sem,
):
    x, y, c, z = place()
    xs = [lax.rem(x + d, NX) for d in range(NX)]
    ys = [lax.rem(y + d, NY) for d in range(NY)]
    zs = [lax.rem(z + d, NZ) for d in range(NZ)]
    sibling = device(x, y, 1 - c, z)
    barrier = pltpu.get_barrier_semaphore()
    peers = [sibling]
    peers += [
        device(xs[dx], ys[dy], c, z) for dx in range(NX) for dy in range(NY) if dx or dy
    ]
    peers += [device(x, y, c, zs[d]) for d in range(1, NZ)]
    halves = (pl.ds(0, HALF), pl.ds(HALF, HALF))
    pairs = [
        (cand_hbm.at[0, halves[0]], cand_rows.at[halves[0]]),
        (input_gain_hbm, input_gain),
        (proj_hbm.at[1], proj.at[1]),
        (cand_hbm.at[0, halves[1]], cand_rows.at[halves[1]]),
        (proj_hbm.at[0], proj.at[0]),
        (user_hbm, user_row),
        (block_hbm, block_row),
        (length_hbm, length_row),
        (cache_hbm.at[:, 0], cache),
        (attention_gain_hbm, attention_gain),
        (weight_hbm, weight),
    ]
    loads = [
        pltpu.make_async_copy(src, dst, load_sem.at[i]) for i, (src, dst) in enumerate(pairs)
    ]
    for load in loads[:8]:
        load.start()
    for peer in peers:
        pl.semaphore_signal(barrier, inc=1, device_id=peer, device_id_type=MESH)

    query = (query_a, query_b)
    sums = (sums_a, sums_b)
    quarters = (pl.ds(0, QUARTER), pl.ds(QUARTER, QUARTER))
    def go(src, dst, recv_sem, peer):
        remote(src, dst, send_sem.at[0], recv_sem, peer).start()

    def arrived(ref, recv_sem):
        remote(ref, ref, send_sem.at[0], recv_sem, sibling).wait_recv()

    def project_query(h):
        loads[3 * h].wait()
        for part in range(2):
            rows = pl.ds(h * HALF + part * QUARTER, QUARTER)
            normed[rows, :] = layer_norm(
                cand_rows[rows, :].astype(F32), input_gain[...]
            ).astype(BF16)
        if h == 0:
            loads[2].wait()
        query[h][x, y, c] = silu(
            jnp.dot(normed[halves[h], :], proj[1], preferred_element_type=F32)
        ).astype(BF16)

    def send_line(h):
        for d in (2, 1, 3):
            for s in range(2):
                peer = device(xs[d], y, c, z) if s == 0 else device(x, ys[d], c, z)
                own = query[h].at[x, y, c, quarters[s]]
                go(own, own, line_recv.at[h, s], peer)

    def to_core(h, block):
        go(block, block, share_recv.at[h], sibling)

    def send_cross(h):
        for s in range(2):
            arrived(query[h].at[pl.ds(0, NX - 1), 0, 0, quarters[s]], line_recv.at[h, s])
            block = (
                query[h].at[:, y, c, quarters[s]] if s == 0 else query[h].at[x, :, c, quarters[s]]
            )
            for d in (2, 1, 3):
                peer = device(x, ys[d], c, z) if s == 0 else device(xs[d], y, c, z)
                go(block, block, cross_recv.at[h, s, d - 1], peer)
            to_core(h, block)

    def share_cross(h):
        for d in (1, 3, 2):
            for s in range(2):
                if s == 0:
                    block = query[h].at[:, ys[NY - d], c, quarters[s]]
                else:
                    block = query[h].at[xs[NX - d], :, c, quarters[s]]
                arrived(block, cross_recv.at[h, s, d - 1])
                to_core(h, block)

    def wait_query(h):
        arrived(query[h].at[:, :, 0], share_recv.at[h])

    loads[1].wait()
    project_query(0)
    pl.semaphore_wait(barrier, len(peers))
    send_line(0)
    project_query(1)
    send_line(1)
    loads[4].wait()
    gate_all[z] = silu(jnp.dot(normed[...], proj[0], preferred_element_type=F32)).astype(BF16)
    for d in HEADS_FAR_FIRST:
        own = gate_all.at[z]
        go(own, own, gate_recv.at[0], device(x, y, c, zs[d]))
    for load in loads[8:]:
        load.start()
    for load in loads[5:8]:
        load.wait()
    sort_slots(user_row[...], block_row[...], length_row[...], table_rows)
    to_scalars = pltpu.make_async_copy(table_rows, table, load_sem.at[len(pairs)])
    to_scalars.start()
    send_cross(0)
    for h in range(2):
        sums[h][SLOTS_HERE] = jnp.zeros((HALF, DH), BF16)
    total[...] = jnp.zeros((HALF, DH), F32)
    to_scalars.wait()
    loads[8].wait()
    share_cross(0)
    send_cross(1)
    wait_query(0)

    def chip_user(kx, ky, which):
        return (kx * NY + ky) * 2 + which

    def part(h, p):
        size = HALF // PARTS[h]
        return pl.ds(p * size, size)

    def send_core(h, p):
        rows = part(h, p)
        for kx in range(NX):
            for ky in range(NY):
                user = chip_user(kx, ky, 1 - c)
                core_out[h, kx, ky, rows] = sums[h][table[LAST, user], rows]
        go(
            core_out.at[h, :, :, rows],
            core_in.at[h, :, :, rows],
            core_recv.at[PARTS[0] * h + p],
            sibling,
        )

    def send_peers(h, p):
        rows = part(h, p)
        arrived(core_in.at[h, :, :, rows], core_recv.at[PARTS[0] * h + p])
        for dx in FAR_FIRST:
            kx = xs[dx]
            for dy in FAR_FIRST:
                mine = sums[h][table[LAST, chip_user(kx, ys[dy], c)], rows]
                peer_out[h, dx * NY + dy, rows] = mine + core_in[h, kx, ys[dy], rows]
            for dy in FAR_FIRST:
                offset = dx * NY + dy
                if offset:
                    go(
                        peer_out.at[h, offset, rows],
                        peer_in.at[h, offset, rows],
                        peer_recv.at[PARTS[0] * h + p],
                        device(kx, ys[dy], c, z),
                    )

    def send_heads(h, p):
        rows = part(h, p)
        arrived(peer_in.at[h, pl.ds(1, NX * NY - 1), rows], peer_recv.at[PARTS[0] * h + p])
        value = peer_out[h, 0, rows].astype(F32)
        for offset in range(1, NX * NY):
            value += peer_in[h, offset, rows].astype(F32)
        attention[h, z, rows] = value.astype(BF16)
        own = attention.at[h, z, rows]
        for d in HEADS_FAR_FIRST:
            go(own, own, head_recv.at[PARTS[0] * h + p], device(x, y, c, zs[d]))

    def finish(h, p):
        rows = part(h, p)
        arrived(attention.at[h, pl.ds(0, NZ - 1), rows], head_recv.at[PARTS[0] * h + p])
        out_rows = pl.ds(h * HALF + rows.start, rows.size)
        whole = jnp.concatenate([attention[h, k, rows].astype(F32) for k in range(NZ)], axis=1)
        gate = jnp.concatenate([gate_all[k, out_rows].astype(F32) for k in range(NZ)], axis=1)
        gated = (layer_norm(whole, attention_gain[...]) * gate).astype(BF16)
        projected = jnp.dot(gated, weight[...], preferred_element_type=F32)
        cols = cand_rows[out_rows, pl.ds(pl.multiple_of(z * DH, DH), DH)].astype(F32)
        result[0, out_rows, :] = (cols + projected).astype(BF16)

    flat_a = query_a.reshape(USERS, HALF, DH)
    flat_b = query_b.reshape(USERS, HALF, DH)
    attend(table, flat_a, cache, sums_a, total, 0, 3)
    share_cross(1)
    attend(table, flat_a, cache, sums_a, total, 3, ROUNDS)
    send_core(0, 0)
    send_core(0, 1)
    wait_query(1)
    total[...] = jnp.zeros((HALF, DH), F32)
    attend(table, flat_b, cache, sums_b, total, 0, 1)
    send_peers(0, 0)
    attend(table, flat_b, cache, sums_b, total, 1, 2)
    send_peers(0, 1)
    attend(table, flat_b, cache, sums_b, total, 2, ROUNDS)
    for p in range(PARTS[1]):
        send_core(1, p)
    send_heads(0, 0)
    send_peers(1, 0)
    send_peers(1, 1)
    send_heads(0, 1)
    send_peers(1, 2)
    send_peers(1, 3)
    loads[9].wait()
    loads[10].wait()
    arrived(gate_all.at[pl.ds(0, NZ - 1)], gate_recv.at[0])
    finish(0, 0)
    send_heads(1, 0)
    send_heads(1, 1)
    send_heads(1, 2)
    finish(0, 1)
    send_heads(1, 3)
    for p in range(PARTS[1]):
        finish(1, p)
    whole = cache.at[pl.ds(0, 19)]
    remote(whole, whole, send_sem.at[0], gate_recv.at[0], sibling).wait_send()


def local(
    candidates,
    input_gain,
    proj_weight,
    history_cache,
    slot_user,
    slot_block,
    history_len,
    attention_gain,
    out_weight,
):
    dma = pltpu.SemaphoreType.DMA
    vmem = pltpu.VMEM
    operands = (
        candidates,
        input_gain.reshape(1, D),
        proj_weight,
        history_cache,
        slot_user.reshape(1, SLOTS_HERE),
        slot_block.reshape(1, SLOTS_HERE),
        history_len.reshape(1, USERS),
        attention_gain.reshape(1, D),
        out_weight,
    )
    return pl.pallas_call(
        kernel,
        out_shape=jax.ShapeDtypeStruct((1, CANDS, DH), BF16),
        in_specs=[pl.BlockSpec(memory_space=pl.ANY)] * len(operands),
        out_specs=pl.BlockSpec(memory_space=vmem),
        scratch_shapes=[
            vmem((CANDS, D), BF16),
            vmem((1, D), F32),
            vmem((2, D, DH), BF16),
            vmem((SLOTS_HERE, BLK, 2 * DH), BF16),
            vmem((1, SLOTS_HERE), I32),
            vmem((1, SLOTS_HERE), I32),
            vmem((1, USERS), I32),
            vmem((1, D), F32),
            vmem((D, DH), BF16),
            vmem((CANDS, D), BF16),
            vmem((NX, NY, 2, HALF, DH), BF16),
            vmem((NX, NY, 2, HALF, DH), BF16),
            vmem((NZ, CANDS, DH), BF16),
            vmem((8, 128), I32),
            pltpu.SMEM((8, 128), I32),
            vmem((SLOTS_HERE + 1, HALF, DH), BF16),
            vmem((SLOTS_HERE + 1, HALF, DH), BF16),
            vmem((HALF, DH), F32),
            vmem((2, NX, NY, HALF, DH), BF16),
            vmem((2, NX, NY, HALF, DH), BF16),
            vmem((2, NX * NY, HALF, DH), BF16),
            vmem((2, NX * NY, HALF, DH), BF16),
            vmem((2, NZ, HALF, DH), BF16),
            dma((len(operands) + 3,)),
            dma((2, 2)),
            dma((2, 2, NX - 1)),
            dma((2,)),
            dma((1,)),
            dma((sum(PARTS),)),
            dma((sum(PARTS),)),
            dma((sum(PARTS),)),
            dma((1,)),
        ],
        compiler_params=pltpu.CompilerParams(
            collective_id=0, has_side_effects=True, vmem_limit_bytes=48 << 20
        ),
        name="layer",
    )(*[pltpu.with_memory_space_constraint(operand, pltpu.HBM) for operand in operands])


def solution(mesh):
    return jax.shard_map(
        local,
        mesh=mesh,
        in_specs=(
            P("cand", None, None),
            P(),
            P(None, None, "hist"),
            P("cand", "hist", None, None),
            P("cand"),
            P("cand"),
            P(),
            P(),
            P(None, "hist"),
        ),
        out_specs=P("cand", None, "hist"),
        check_vma=False,
    )
```
